768 devices in a mesh: dp: 12 (over x, z_hi), tensor: 64 (over y, z_lo, core).
Axes of the slice: x: 4, y: 8, z: 12 (z_hi: 3, z_lo: 4; z = z_hi * 4 + z_lo), core: 2. Of those that a mesh axis runs over, the one named last changes fastest.
Arguments:
- tokens: bfloat16 [3072, 4096], P(('dp', 'tensor')), may hold values from -6 to 6
- norm_gain: bfloat16 [4096], replicated, may hold values from 0.099609375 to 1.8984375
- gate_weight: bfloat16 [4096, 14336], P(None, 'tensor'), may hold values from -0.09375 to 0.09375
- up_weight: bfloat16 [4096, 14336], P(None, 'tensor'), may hold values from -0.09375 to 0.09375
- down_weight: bfloat16 [14336, 4096], P('tensor'), may hold values from -0.046875 to 0.046875
- drop_mask: int32 [3072, 4096], P(('dp', 'tensor')), may hold values 0 or 1
- grad_bucket: bfloat16 [12, 16384, 1536], P('dp', 'tensor'), may hold values from -6 to 6
Outputs:
- mixed: bfloat16 [3072, 4096], P(('dp', 'tensor'))
- reduced: float32 [16384, 1536], P('tensor', 'dp')
The draws below stay inside these ranges and needn't reach their ends.
All inputs are finite; a program needn't handle non-finite values. No bound on the sum of `drop_mask` on one device may be relied on, other than what follows from the above.
Results may differ from the reference program's by a relative error of at most 0.012.
Values may be sent and summed in bfloat16 or wider, within the bound.
No kernel may reach another device: no remote copies, remote signals or barrier semaphores. Data moves between devices by JAX's collectives and lax.ppermute only.
A program may use at most 64 MiB of HBM per device.

```python
import jax
import jax.numpy as jnp
from jax import lax

D = 4096
FF = 14336
TOKENS = 3072
GROWS = 16384
GCOLS = 1536
N_DP = 12


def touch_ends(drawn, key, smallest, high):
    extent = drawn.shape
    index_at = [jax.random.randint(jax.random.fold_in(key, axis), (), 0, extent[axis]) for axis in range(len(extent))]
    drawn = drawn.at[tuple(index_at)].set(smallest)
    longest = extent.index(max(extent))
    index_at[longest] = (index_at[longest] + 1) % extent[longest]
    return drawn.at[tuple(index_at)].set(high)


def level_of(key, shape, cuts, low, top_value):
    def one(dim, blocks):
        steps = jax.random.uniform(jax.random.fold_in(jax.random.fold_in(key, 6), dim), (blocks,), jnp.float32, low / len(cuts), top_value / len(cuts))
        return jnp.repeat(jnp.exp(steps), shape[dim] // blocks).reshape((-1,) + (1,) * (len(shape) - dim - 1))

    loudness = one(*cuts[0])
    for cut in cuts[1:]:
        loudness = loudness * one(*cut)
    return loudness


def bell_draw(own_key, dims, width, most, pieces=(), held_as=jnp.bfloat16):
    gain = level_of(own_key, dims, pieces, -0.22, 0.18) if pieces else 1.0
    entries = jax.random.normal(own_key, dims, jnp.float32) * width * gain
    return jnp.minimum(jnp.maximum(entries, -most), most).astype(held_as)


def setup_inputs(seed: int = 0) -> dict:
    key_of = jax.random.split(jax.random.key(seed), 8)
    tokens = bell_draw(key_of[0], (TOKENS, D), 1.0, 6.0, ((0, 768),))
    norm_gain = jnp.clip(1.0 + 0.18 * jax.random.normal(key_of[1], (D,), jnp.float32), 0.099609375, 1.8984375).astype(jnp.bfloat16)
    gate_weight = bell_draw(key_of[2], (D, FF), D ** -0.5, 0.09375, ((1, 64),))
    up_weight = bell_draw(key_of[3], (D, FF), D ** -0.5, 0.09375, ((1, 64),))
    down_weight = bell_draw(key_of[4], (FF, D), FF ** -0.5, 0.046875, ((0, 64),))
    drop_mask = touch_ends((jax.random.randint(key_of[5], (TOKENS, D), 0, 10) < 9).astype(jnp.int32), jax.random.fold_in(key_of[5], 1), 0, 1)
    grad_bucket = bell_draw(key_of[6], (N_DP, GROWS, GCOLS), 1.0, 6.0, ((0, 12), (1, 64)))
    return dict(tokens=tokens, norm_gain=norm_gain, gate_weight=gate_weight, up_weight=up_weight, down_weight=down_weight, drop_mask=drop_mask, grad_bucket=grad_bucket)


def reference(tokens, norm_gain, gate_weight, up_weight, down_weight, drop_mask, grad_bucket):
    inputs = tokens.astype(jnp.float32)
    scale = lax.rsqrt(lax.optimization_barrier(jnp.mean(inputs * inputs, axis=-1, keepdims=True)) + 1e-05)
    normed = (inputs * scale * norm_gain.astype(jnp.float32)).astype(jnp.bfloat16)
    gate = jnp.dot(normed, gate_weight, preferred_element_type=jnp.float32)
    up_part = jnp.dot(normed, up_weight, preferred_element_type=jnp.float32)
    hidden = (jax.nn.silu(gate) * up_part).astype(jnp.bfloat16)
    branch = jnp.dot(hidden, down_weight, preferred_element_type=jnp.float32)
    mixed = (inputs + drop_mask.astype(jnp.float32) * branch / 0.9).astype(jnp.bfloat16)
    reduced = lax.optimization_barrier(jnp.sum(grad_bucket.astype(jnp.float32), axis=0))
    return (mixed, reduced)
```

```python
import functools

import jax
import jax.numpy as jnp
from jax import lax
from jax.experimental import pallas as pl
from jax.experimental.pallas import tpu as pltpu
from jax.sharding import Mesh
from jax.sharding import PartitionSpec as P

DP = ("x", "zh")
TENSOR = ("y", "zl", "c")
BF16, F32 = jnp.bfloat16, jnp.float32
EPS = 1e-05
KEEP = 0.9


def call(body, outs, *args, smem=0, scratch=(), vmem=32, flops=0, moved=1 << 20):
    whole = pl.BlockSpec(memory_space=pltpu.VMEM)
    return pl.pallas_call(
        body,
        out_shape=outs,
        in_specs=[pl.BlockSpec(memory_space=pltpu.SMEM)] * smem + [whole] * (len(args) - smem),
        out_specs=jax.tree.map(lambda _: whole, outs),
        scratch_shapes=list(scratch),
        compiler_params=pltpu.CompilerParams(vmem_limit_bytes=vmem << 20),
        cost_estimate=pl.CostEstimate(flops=flops, bytes_accessed=moved, transcendentals=0),
    )(*args)


def norm_body(tok_ref, gain_ref, out_ref):
    few, wide = tok_ref.shape
    quarter = wide // 4
    inputs = tok_ref[...].astype(F32)
    scale = lax.rsqrt(jnp.mean(inputs * inputs, axis=-1, keepdims=True) + EPS)
    normed = inputs * scale * gain_ref[...].astype(F32)
    for half in range(2):
        at = 2 * half * quarter
        block = jnp.concatenate(
            [normed[:, at : at + quarter], normed[:, at + quarter : at + 2 * quarter]], axis=0
        ).astype(BF16)
        for i in range(out_ref.shape[0] // 2):
            out_ref[2 * i + half] = block


def paired(first, second):
    upper = lax.broadcasted_iota(jnp.int32, first.shape, 1) < first.shape[1] // 2
    turn = first.shape[1] // 2
    return (
        jnp.where(upper, first, pltpu.roll(second, turn, 1)),
        jnp.where(upper, pltpu.roll(first, turn, 1), second),
    )


def dot_t(x, w):
    return lax.dot_general(x, w, (((1,), (1,)), ((), ())), preferred_element_type=F32)


def halves(x_ref):
    blocks, eight, quarter = x_ref.shape
    x = x_ref[...].astype(F32).reshape(blocks // 2, 2, eight, quarter)
    first, second = paired(x[:, 0], x[:, 1])
    rows = blocks * eight // 2
    return first.reshape(rows, quarter).astype(BF16), second.reshape(rows, quarter).astype(BF16)


def lead_body(core_ref, x_ref, gate_ref, up_ref, gate_out, up_out):
    quarter = x_ref.shape[-1]
    at = pl.multiple_of(core_ref[0] * (2 * quarter), 2 * quarter)
    first, second = halves(x_ref)
    for w_ref, out in ((gate_ref, gate_out), (up_ref, up_out)):
        part = dot_t(first, w_ref[:, pl.ds(at, quarter)])
        out[...] = part + dot_t(second, w_ref[:, pl.ds(at + quarter, quarter)])


def hidden_body(core_ref, x_ref, gate_ref, up_ref, down_ref, gate_in, up_in, hid_out, far_out):
    quarter = x_ref.shape[-1]
    at = pl.multiple_of((1 - core_ref[0]) * (2 * quarter), 2 * quarter)
    first, second = halves(x_ref)

    def both(w_ref, part_ref):
        part = part_ref[...] + dot_t(first, w_ref[:, pl.ds(at, quarter)])
        return part + dot_t(second, w_ref[:, pl.ds(at + quarter, quarter)])

    gate = both(gate_ref, gate_in)
    up = both(up_ref, up_in)
    hidden = (gate / (1.0 + jnp.exp(-gate)) * up).astype(BF16)
    hid_out[...] = hidden
    for k in range(4):
        cols = pl.ds(at + k * (quarter // 2), quarter // 2)
        out = jnp.dot(hidden, down_ref[:, cols], preferred_element_type=F32)
        far_out[:, k * (quarter // 2) : (k + 1) * (quarter // 2)] = out.astype(BF16)


def down_body(core_ref, hid_ref, down_ref, near_ref, out_ref):
    blocks, eight, quarter = out_ref.shape
    at = pl.multiple_of(core_ref[0] * (2 * quarter), 2 * quarter)
    hidden = hid_ref[...]
    step = quarter // 2
    for k in range(2):
        sums = []
        for q in range(2):
            here = q * quarter + k * step
            part = jnp.dot(hidden, down_ref[:, pl.ds(at + here, step)], preferred_element_type=F32)
            part += near_ref[:, here : here + step].astype(F32)
            sums.append(part.reshape(blocks // 2, eight, step))
        both = jnp.stack(paired(*sums), axis=1)
        out_ref[:, :, k * step : (k + 1) * step] = both.reshape(blocks, eight, step).astype(BF16)


def final_body(in_ref, tok_ref, mask_ref, out_ref):
    few, wide = tok_ref.shape
    quarter = wide // 4
    for half in range(2):
        total = in_ref[half].astype(F32)
        for i in range(1, in_ref.shape[0] // 2):
            total = total + in_ref[2 * i + half].astype(F32)
        for q in range(2):
            cols = slice((2 * half + q) * quarter, (2 * half + q + 1) * quarter)
            branch = total[q * few : (q + 1) * few]
            kept = mask_ref[:, cols].astype(F32) * branch / KEEP
            out_ref[:, cols] = (tok_ref[:, cols].astype(F32) + kept).astype(BF16)


def cut_body(place_ref, in_ref, *outs):
    width = outs[0].shape[1]
    for k, out in enumerate(outs):
        at = lax.rem(place_ref[0] + k, len(outs)) * width
        out[...] = in_ref[:, pl.ds(pl.multiple_of(at, width), width)]


def sum_cut_body(place_ref, *refs, terms):
    total = refs[0][...].astype(F32)
    for ref in refs[1:terms]:
        total = total + ref[...].astype(F32)
    outs, held = refs[terms:-1], refs[-1]
    held[...] = total
    width = outs[0].shape[1]
    for k, out in enumerate(outs):
        at = lax.rem(place_ref[0] + k, len(outs)) * width
        out[...] = held[:, pl.ds(pl.multiple_of(at, width), width)].astype(out.dtype)


def sum_body(*refs):
    total = refs[0][...].astype(F32)
    for ref in refs[1:-1]:
        total = total + ref[...].astype(F32)
    refs[-1][...] = total


def shape(*dims, dtype=BF16):
    return jax.ShapeDtypeStruct(dims, dtype)


def place(axis):
    return lax.axis_index(axis).astype(jnp.int32).reshape(1)


def passed_on(x, axis, by):
    size = lax.axis_size(axis)
    return lax.ppermute(x, axis, [(i, (i + by) % size) for i in range(size)])


def bucket_sum(bucket):
    rows, cols = bucket.shape
    nx, nh = lax.axis_size("x"), lax.axis_size("zh")
    wide, narrow = cols // nx, cols // nx // nh
    cut = call(cut_body, (shape(rows, wide),) * nx, place("x"), bucket, smem=1)
    terms = [cut[0]] + [passed_on(cut[k], "x", k) for k in range(1, nx)]
    cut = call(
        functools.partial(sum_cut_body, terms=nx),
        (shape(rows, narrow),) * nh,
        place("zh"), *terms,
        smem=1, scratch=[pltpu.VMEM((rows, wide), F32)],
    )
    terms = [cut[0]] + [passed_on(cut[k], "zh", k) for k in range(1, nh)]
    return call(sum_body, shape(rows, narrow, dtype=F32), *terms)


def per_device(tokens, norm_gain, gate_weight, up_weight, down_weight, drop_mask, grad_bucket):
    few, wide = tokens.shape
    quarter = wide // 4
    group = lax.axis_size(TENSOR)
    rows = group * few
    units = gate_weight.shape[1]
    core = place("c")
    gate_weight, up_weight = gate_weight.T, up_weight.T
    blocks = shape(group, 2 * few, quarter)
    part = shape(rows, units, dtype=F32)

    reduced = bucket_sum(grad_bucket[0])

    own = call(norm_body, blocks, tokens, norm_gain.reshape(1, wide))
    own = lax.all_to_all(own, TENSOR, 0, 0, tiled=True)
    far = passed_on(own, "c", 1)
    gate, up = call(
        lead_body, (part, part), core, own, gate_weight, up_weight,
        smem=1, flops=2 * rows * wide * units,
    )
    hidden, send = call(
        hidden_body,
        (shape(rows, units), shape(rows, 2 * quarter)),
        core, far, gate_weight, up_weight, down_weight, gate, up,
        smem=1, flops=3 * rows * wide * units,
    )
    near = passed_on(send, "c", 1)
    terms = call(down_body, blocks, core, hidden, down_weight, near, smem=1, flops=rows * wide * units)
    terms = lax.all_to_all(terms, TENSOR, 0, 0, tiled=True)
    mixed = call(final_body, shape(few, wide), terms, tokens, drop_mask)
    return (mixed, reduced)


def solution(mesh):
    finer = Mesh(mesh.devices.reshape(4, 3, 8, 4, 2), DP + TENSOR)
    return jax.shard_map(
        per_device,
        mesh=finer,
        in_specs=(
            P(DP + TENSOR, None),
            P(),
            P(None, TENSOR),
            P(None, TENSOR),
            P(TENSOR, None),
            P(DP + TENSOR, None),
            P(DP, TENSOR, None),
        ),
        out_specs=(P(DP + TENSOR, None), P(TENSOR, DP)),
        check_vma=False,
    )
```

```python
import functools

import jax
import jax.numpy as jnp
from jax import lax
from jax.experimental import pallas as pl
from jax.experimental.pallas import tpu as pltpu
from jax.sharding import Mesh
from jax.sharding import PartitionSpec as P

DP = ("x", "zh")
CHIPS = ("y", "zl")
TENSOR = CHIPS + ("c",)
BF16, F32 = jnp.bfloat16, jnp.float32
EPS = 1e-05
KEEP = 0.9


def call(body, outs, *args, smem=0, hbm=0, scratch=(), vmem=16, flops=0, moved=1 << 20):
    whole = pl.BlockSpec(memory_space=pltpu.VMEM)
    specs = [pl.BlockSpec(memory_space=pltpu.SMEM)] * smem
    specs += [whole] * (len(args) - smem - hbm)
    specs += [pl.BlockSpec(memory_space=pltpu.HBM)] * hbm
    return pl.pallas_call(
        body,
        out_shape=outs,
        in_specs=specs,
        out_specs=jax.tree.map(lambda _: whole, outs),
        scratch_shapes=list(scratch),
        compiler_params=pltpu.CompilerParams(vmem_limit_bytes=vmem << 20),
        cost_estimate=pl.CostEstimate(flops=flops, bytes_accessed=moved, transcendentals=0),
    )(*args)


def brought(pairs, sems):
    copies = [pltpu.make_async_copy(a, b, sems.at[i]) for i, (a, b) in enumerate(pairs)]
    for copy in copies:
        copy.start()
    return copies


def norm_body(tok_hbm, gain_hbm, out_ref, tok_ref, gain_ref, sems):
    half = tok_ref.shape[1] // 2
    for copy in brought(((tok_hbm, tok_ref), (gain_hbm, gain_ref)), sems):
        copy.wait()
    inputs = tok_ref[...].astype(F32)
    scale = lax.rsqrt(jnp.mean(inputs * inputs, axis=-1, keepdims=True) + EPS)
    normed = inputs * scale * gain_ref[...].astype(F32)[None, :]
    block = jnp.concatenate([normed[:, :half], normed[:, half:]], axis=0).astype(BF16)
    for i in range(out_ref.shape[0]):
        out_ref[i] = block


def paired(first, second):
    upper = lax.broadcasted_iota(jnp.int32, first.shape, 1) < first.shape[1] // 2
    turn = first.shape[1] // 2
    return (
        jnp.where(upper, first, pltpu.roll(second, turn, 1)),
        jnp.where(upper, pltpu.roll(first, turn, 1), second),
    )


def dot_t(x, w):
    return lax.dot_general(x, w, (((1,), (1,)), ((), ())), preferred_element_type=F32)


def ffn_body(x_ref, *refs):
    sent, out_ref, held, sems = refs[:6], refs[6], refs[7:13], refs[13]
    down_a, down_b = held[4:]
    copies = brought(list(zip(sent, held)), sems)
    blocks, eight, half = x_ref.shape
    rows = blocks * eight // 2
    x = x_ref[...].astype(F32).reshape(blocks // 2, 2, eight, half)
    left, right = (v.reshape(rows, half).astype(BF16) for v in paired(x[:, 0], x[:, 1]))

    def through(at):
        copies[at].wait()
        w_ref = held[at]
        return dot_t(left, w_ref[:, :half]) + dot_t(right, w_ref[:, half:])

    gates = [through(0), through(1)]
    ups = [through(2), through(3)]
    hidden = [(gate / (1.0 + jnp.exp(-gate)) * up).astype(BF16) for gate, up in zip(gates, ups)]
    copies[4].wait()
    copies[5].wait()
    step = min(half, 512)
    for k in range(half // step):
        sums = []
        for cols in (slice(k * step, (k + 1) * step), slice(half + k * step, half + (k + 1) * step)):
            part = jnp.dot(hidden[0], down_a[:, cols], preferred_element_type=F32)
            part += jnp.dot(hidden[1], down_b[:, cols], preferred_element_type=F32)
            sums.append(part.reshape(blocks // 2, eight, step))
        both = jnp.stack(paired(*sums), axis=1)
        out_ref[:, :, k * step : (k + 1) * step] = both.reshape(blocks, eight, step).astype(BF16)


def final_body(in_ref, tok_ref, mask_ref, out_ref):
    few, wide = tok_ref.shape
    half = wide // 2
    total = in_ref[0].astype(F32)
    for i in range(1, in_ref.shape[0]):
        total = total + in_ref[i].astype(F32)
    for q in range(2):
        cols = slice(q * half, (q + 1) * half)
        branch = total[q * few : (q + 1) * few]
        kept = mask_ref[:, cols].astype(F32) * branch / KEEP
        out_ref[:, cols] = (tok_ref[:, cols].astype(F32) + kept).astype(BF16)


def cut_body(place_ref, in_hbm, *refs):
    outs, sems = refs[:-1], refs[-1]
    width = outs[0].shape[1]
    pairs = []
    for k, out in enumerate(outs):
        at = lax.rem(place_ref[0] + k, len(outs)) * width
        pairs.append((in_hbm.at[:, pl.ds(pl.multiple_of(at, width), width)], out))
    for copy in brought(pairs, sems):
        copy.wait()


def sum_cut_body(place_ref, *refs, terms):
    total = refs[0][...].astype(F32)
    for ref in refs[1:terms]:
        total = total + ref[...].astype(F32)
    outs, held = refs[terms:-1], refs[-1]
    held[...] = total
    width = outs[0].shape[1]
    for k, out in enumerate(outs):
        at = lax.rem(place_ref[0] + k, len(outs)) * width
        out[...] = held[:, pl.ds(pl.multiple_of(at, width), width)].astype(out.dtype)


def sum_first_body(in_ref, out_ref):
    rows = 16
    for r in range(0, out_ref.shape[0], rows):
        total = in_ref[0, r : r + rows].astype(F32)
        for i in range(1, in_ref.shape[0]):
            total = total + in_ref[i, r : r + rows].astype(F32)
        out_ref[r : r + rows] = total.astype(BF16)


def sum_body(*refs):
    total = refs[0][...].astype(F32)
    for ref in refs[1:-1]:
        total = total + ref[...].astype(F32)
    refs[-1][...] = total


def shape(*dims, dtype=BF16):
    return jax.ShapeDtypeStruct(dims, dtype)


def place(axis):
    return lax.axis_index(axis).astype(jnp.int32).reshape(1)


def passed_on(x, axis, by):
    size = lax.axis_size(axis)
    return lax.ppermute(x, axis, [(i, (i + by) % size) for i in range(size)])


def bucket_over_x(bucket):
    rows, cols = bucket.shape
    nx = lax.axis_size("x")
    cut = call(
        cut_body, (shape(rows, cols // nx),) * nx, place("x"), bucket,
        smem=1, hbm=1, vmem=60, scratch=[pltpu.SemaphoreType.DMA((nx,))],
    )
    return [cut[0]] + [passed_on(cut[k], "x", k) for k in range(1, nx)]


def bucket_cut(terms):
    rows, wide = terms[0].shape
    nh = lax.axis_size("zh")
    return call(
        functools.partial(sum_cut_body, terms=len(terms)),
        (shape(rows, wide // nh),) * nh,
        place("zh"), *terms,
        smem=1, scratch=[pltpu.VMEM((rows, wide), F32)],
    )


def per_device(tokens, norm_gain, gate_weight, up_weight, down_weight, drop_mask, grad_bucket):
    few, wide = tokens.shape
    chips = lax.axis_size(CHIPS)
    units = gate_weight.shape[1]
    blocks = shape(chips, 2 * few, wide // 2)

    gathered = call(
        norm_body, blocks, tokens, norm_gain,
        hbm=2, vmem=60,
        scratch=[
            pltpu.VMEM(tokens.shape, BF16),
            pltpu.VMEM(norm_gain.shape, BF16),
            pltpu.SemaphoreType.DMA((2,)),
        ],
    )
    gathered = lax.all_to_all(gathered, CHIPS, 0, 0, tiled=True)
    bucket = bucket_over_x(grad_bucket[0])
    down_weight, bucket[1] = lax.optimization_barrier((down_weight, bucket[1]))
    weights = []
    for mine in (gate_weight.T, up_weight.T, down_weight):
        weights += [mine, passed_on(mine, "c", 1)]
    cut = bucket_cut(bucket)
    gathered, cut = lax.optimization_barrier((gathered, cut))
    terms = call(
        ffn_body, blocks, gathered, *weights,
        hbm=6,
        scratch=[pltpu.VMEM((units, wide), BF16)] * 6 + [pltpu.SemaphoreType.DMA((6,))],
        vmem=48, flops=12 * chips * few * wide * units, moved=14 * wide * units,
    )
    bucket = [cut[0]] + [passed_on(cut[k], "zh", k) for k in range(1, len(cut))]
    ny, nz = (lax.axis_size(axis) for axis in CHIPS)
    terms = terms.reshape(ny, nz * 2 * few, wide // 2)
    terms = lax.all_to_all(terms, "y", 0, 0, tiled=True)
    terms = call(sum_first_body, shape(nz * 2 * few, wide // 2), terms)
    terms, bucket = lax.optimization_barrier((terms.reshape(nz, 2 * few, wide // 2), bucket))
    terms = lax.all_to_all(terms, "zl", 0, 0, tiled=True)
    reduced = call(sum_body, shape(*cut[0].shape, dtype=F32), *bucket)
    mixed = call(final_body, shape(few, wide), terms, tokens, drop_mask)
    return (mixed, reduced)


def solution(mesh):
    finer = Mesh(mesh.devices.reshape(4, 3, 8, 4, 2), DP + TENSOR)
    return jax.shard_map(
        per_device,
        mesh=finer,
        in_specs=(
            P(DP + TENSOR, None),
            P(),
            P(None, TENSOR),
            P(None, TENSOR),
            P(TENSOR, None),
            P(DP + TENSOR, None),
            P(DP, TENSOR, None),
        ),
        out_specs=(P(DP + TENSOR, None), P(TENSOR, DP)),
        check_vma=False,
    )
```

```python
import functools

import jax
import jax.numpy as jnp
from jax import lax
from jax.experimental import pallas as pl
from jax.experimental.pallas import tpu as pltpu
from jax.sharding import Mesh
from jax.sharding import PartitionSpec as P

DP = ("x", "zh")
CHIPS = ("y", "zl")
TENSOR = CHIPS + ("c",)
BF16, F32 = jnp.bfloat16, jnp.float32
EPS = 1e-05
KEEP = 0.9


def call(body, outs, *args, smem=0, hbm=0, scratch=(), vmem=16, flops=0, moved=1 << 20):
    whole = pl.BlockSpec(memory_space=pltpu.VMEM)
    specs = [pl.BlockSpec(memory_space=pltpu.SMEM)] * smem
    specs += [whole] * (len(args) - smem - hbm)
    specs += [pl.BlockSpec(memory_space=pltpu.HBM)] * hbm
    return pl.pallas_call(
        body,
        out_shape=outs,
        in_specs=specs,
        out_specs=jax.tree.map(lambda _: whole, outs),
        scratch_shapes=list(scratch),
        compiler_params=pltpu.CompilerParams(vmem_limit_bytes=vmem << 20),
        cost_estimate=pl.CostEstimate(flops=flops, bytes_accessed=moved, transcendentals=0),
    )(*args)


def brought(pairs, sems):
    copies = [pltpu.make_async_copy(a, b, sems.at[i]) for i, (a, b) in enumerate(pairs)]
    for copy in copies:
        copy.start()
    return copies


def norm_body(tok_hbm, gain_hbm, out_ref, tok_ref, gain_ref, sems):
    half = tok_ref.shape[1] // 2
    for copy in brought(((tok_hbm, tok_ref), (gain_hbm, gain_ref)), sems):
        copy.wait()
    inputs = tok_ref[...].astype(F32)
    scale = lax.rsqrt(jnp.mean(inputs * inputs, axis=-1, keepdims=True) + EPS)
    normed = inputs * scale * gain_ref[...].astype(F32)[None, :]
    block = jnp.concatenate([normed[:, :half], normed[:, half:]], axis=0).astype(BF16)
    for i in range(out_ref.shape[0]):
        out_ref[i] = block


def paired(first, second):
    upper = lax.broadcasted_iota(jnp.int32, first.shape, 1) < first.shape[1] // 2
    turn = first.shape[1] // 2
    return (
        jnp.where(upper, first, pltpu.roll(second, turn, 1)),
        jnp.where(upper, pltpu.roll(first, turn, 1), second),
    )


def dot_t(x, w):
    return lax.dot_general(x, w, (((1,), (1,)), ((), ())), preferred_element_type=F32)


def ffn_body(x_ref, *refs):
    sent, out_ref, held, sems = refs[:6], refs[6], refs[7:13], refs[13]
    down_a, down_b = held[4:]
    copies = brought(list(zip(sent, held)), sems)
    blocks, eight, half = x_ref.shape
    rows = blocks * eight // 2
    x = x_ref[...].astype(F32).reshape(blocks // 2, 2, eight, half)
    left, right = (v.reshape(rows, half).astype(BF16) for v in paired(x[:, 0], x[:, 1]))

    def through(at):
        copies[at].wait()
        w_ref = held[at]
        return dot_t(left, w_ref[:, :half]) + dot_t(right, w_ref[:, half:])

    gates = [through(0), through(1)]
    ups = [through(2), through(3)]
    hidden = [(gate / (1.0 + jnp.exp(-gate)) * up).astype(BF16) for gate, up in zip(gates, ups)]
    copies[4].wait()
    copies[5].wait()
    step = min(half, 512)
    for k in range(half // step):
        sums = []
        for cols in (slice(k * step, (k + 1) * step), slice(half + k * step, half + (k + 1) * step)):
            part = jnp.dot(hidden[0], down_a[:, cols], preferred_element_type=F32)
            part += jnp.dot(hidden[1], down_b[:, cols], preferred_element_type=F32)
            sums.append(part.reshape(blocks // 2, eight, step))
        both = jnp.stack(paired(*sums), axis=1)
        out_ref[:, :, k * step : (k + 1) * step] = both.reshape(blocks, eight, step).astype(BF16)


def final_body(in_ref, tok_ref, mask_ref, out_ref):
    few, wide = tok_ref.shape
    half = wide // 2
    total = in_ref[0].astype(F32)
    for i in range(1, in_ref.shape[0]):
        total = total + in_ref[i].astype(F32)
    for q in range(2):
        cols = slice(q * half, (q + 1) * half)
        branch = total[q * few : (q + 1) * few]
        kept = mask_ref[:, cols].astype(F32) * branch / KEEP
        out_ref[:, cols] = (tok_ref[:, cols].astype(F32) + kept).astype(BF16)


def cut_body(place_ref, in_hbm, *refs):
    outs, sems = refs[:-1], refs[-1]
    width = outs[0].shape[1]
    pairs = []
    for k, out in enumerate(outs):
        at = lax.rem(place_ref[0] + k, len(outs)) * width
        pairs.append((in_hbm.at[:, pl.ds(pl.multiple_of(at, width), width)], out))
    for copy in brought(pairs, sems):
        copy.wait()


def sum_cut_body(*refs):
    total = refs[0][...].astype(F32)
    for ref in refs[1:-1]:
        total = total + ref[...].astype(F32)
    out_ref = refs[-1]
    width = out_ref.shape[-1]
    for k in range(out_ref.shape[0]):
        out_ref[k] = total[:, k * width : (k + 1) * width].astype(BF16)


def sum_parts_body(in_ref, out_ref):
    total = in_ref[0].astype(F32)
    for k in range(1, in_ref.shape[0]):
        total = total + in_ref[k].astype(F32)
    out_ref[...] = total


def shape(*dims, dtype=BF16):
    return jax.ShapeDtypeStruct(dims, dtype)


def place(axis):
    return lax.axis_index(axis).astype(jnp.int32).reshape(1)


def passed_on(x, axis, by):
    size = lax.axis_size(axis)
    return lax.ppermute(x, axis, [(i, (i + by) % size) for i in range(size)])


def bucket_over_x(bucket):
    rows, cols = bucket.shape
    nx = lax.axis_size("x")
    cut = call(
        cut_body, (shape(rows, cols // nx),) * nx, place("x"), bucket,
        smem=1, hbm=1, vmem=60, scratch=[pltpu.SemaphoreType.DMA((nx,))],
    )
    return [cut[0]] + [passed_on(cut[k], "x", k) for k in range(1, nx)]


def bucket_cut(terms):
    rows, wide = terms[0].shape
    nh = lax.axis_size("zh")
    return call(sum_cut_body, shape(nh, rows, wide // nh), *terms)


def per_device(tokens, norm_gain, gate_weight, up_weight, down_weight, drop_mask, grad_bucket):
    few, wide = tokens.shape
    chips = lax.axis_size(CHIPS)
    units = gate_weight.shape[1]
    blocks = shape(chips, 2 * few, wide // 2)

    gathered = call(
        norm_body, blocks, tokens, norm_gain,
        hbm=2, vmem=60,
        scratch=[
            pltpu.VMEM(tokens.shape, BF16),
            pltpu.VMEM(norm_gain.shape, BF16),
            pltpu.SemaphoreType.DMA((2,)),
        ],
    )
    gathered = lax.all_to_all(gathered, CHIPS, 0, 0, tiled=True)
    bucket = bucket_over_x(grad_bucket[0])
    down_weight, bucket[1] = lax.optimization_barrier((down_weight, bucket[1]))
    weights = []
    for mine in (gate_weight.T, up_weight.T, down_weight):
        weights += [mine, passed_on(mine, "c", 1)]
    cut = bucket_cut(bucket)
    gathered, cut = lax.optimization_barrier((gathered, cut))
    bucket = lax.all_to_all(cut, "zh", 0, 0, tiled=True)
    terms = call(
        ffn_body, blocks, gathered, *weights,
        hbm=6,
        scratch=[pltpu.VMEM((units, wide), BF16)] * 6 + [pltpu.SemaphoreType.DMA((6,))],
        vmem=48, flops=12 * chips * few * wide * units, moved=14 * wide * units,
    )
    terms, bucket = lax.optimization_barrier((terms, bucket))
    terms = lax.all_to_all(terms, CHIPS, 0, 0, tiled=True)
    reduced = call(sum_parts_body, shape(*cut.shape[1:], dtype=F32), bucket)
    mixed = call(final_body, shape(few, wide), terms, tokens, drop_mask)
    return (mixed, reduced)


def solution(mesh):
    finer = Mesh(mesh.devices.reshape(4, 3, 8, 4, 2), DP + TENSOR)
    return jax.shard_map(
        per_device,
        mesh=finer,
        in_specs=(
            P(DP + TENSOR, None),
            P(),
            P(None, TENSOR),
            P(None, TENSOR),
            P(TENSOR, None),
            P(DP + TENSOR, None),
            P(DP, TENSOR, None),
        ),
        out_specs=(P(DP + TENSOR, None), P(TENSOR, DP)),
        check_vma=False,
    )
```

```python
import functools

import jax
import jax.numpy as jnp
from jax import lax
from jax.experimental import pallas as pl
from jax.experimental.pallas import tpu as pltpu
from jax.sharding import Mesh
from jax.sharding import PartitionSpec as P

DP = ("x", "zh")
CHIPS = ("y", "zb", "za")
TENSOR = ("y", "za", "zb", "c")
BF16, F32 = jnp.bfloat16, jnp.float32
EPS = 1e-05
KEEP = 0.9


def call(body, outs, *args, smem=0, hbm=0, scratch=(), vmem=16, flops=0, moved=1 << 20):
    whole = pl.BlockSpec(memory_space=pltpu.VMEM)
    specs = [pl.BlockSpec(memory_space=pltpu.SMEM)] * smem
    specs += [whole] * (len(args) - smem - hbm)
    specs += [pl.BlockSpec(memory_space=pltpu.HBM)] * hbm
    return pl.pallas_call(
        body,
        out_shape=outs,
        in_specs=specs,
        out_specs=jax.tree.map(lambda _: whole, outs),
        scratch_shapes=list(scratch),
        compiler_params=pltpu.CompilerParams(vmem_limit_bytes=vmem << 20),
        cost_estimate=pl.CostEstimate(flops=flops, bytes_accessed=moved, transcendentals=0),
    )(*args)


def brought(pairs, sems):
    copies = [pltpu.make_async_copy(a, b, sems.at[i]) for i, (a, b) in enumerate(pairs)]
    for copy in copies:
        copy.start()
    return copies


def norm_body(tok_hbm, gain_hbm, out_ref, tok_ref, gain_ref, sems):
    half = tok_ref.shape[1] // 2
    for copy in brought(((tok_hbm, tok_ref), (gain_hbm, gain_ref)), sems):
        copy.wait()
    inputs = tok_ref[...].astype(F32)
    scale = lax.rsqrt(jnp.mean(inputs * inputs, axis=-1, keepdims=True) + EPS)
    normed = inputs * scale * gain_ref[...].astype(F32)[None, :]
    block = jnp.concatenate([normed[:, :half], normed[:, half:]], axis=0).astype(BF16)
    for i in range(out_ref.shape[0]):
        out_ref[i] = block


def paired(first, second):
    upper = lax.broadcasted_iota(jnp.int32, first.shape, 1) < first.shape[1] // 2
    turn = first.shape[1] // 2
    return (
        jnp.where(upper, first, pltpu.roll(second, turn, 1)),
        jnp.where(upper, pltpu.roll(first, turn, 1), second),
    )


def dot_t(x, w):
    return lax.dot_general(x, w, (((1,), (1,)), ((), ())), preferred_element_type=F32)


def ffn_body(x_ref, *refs):
    sent, out_ref, held, sems = refs[:6], refs[6], refs[7:13], refs[13]
    down_a, down_b = held[4:]
    copies = brought(list(zip(sent, held)), sems)
    blocks, eight, half = x_ref.shape
    rows = blocks * eight // 2
    x = x_ref[...].astype(F32).reshape(blocks // 2, 2, eight, half)
    left, right = (v.reshape(rows, half).astype(BF16) for v in paired(x[:, 0], x[:, 1]))

    def through(at):
        copies[at].wait()
        w_ref = held[at]
        return dot_t(left, w_ref[:, :half]) + dot_t(right, w_ref[:, half:])

    gates = [through(0), through(1)]
    ups = [through(2), through(3)]
    hidden = [(gate / (1.0 + jnp.exp(-gate)) * up).astype(BF16) for gate, up in zip(gates, ups)]
    copies[4].wait()
    copies[5].wait()
    step = min(half, 512)
    for k in range(half // step):
        sums = []
        for cols in (slice(k * step, (k + 1) * step), slice(half + k * step, half + (k + 1) * step)):
            part = jnp.dot(hidden[0], down_a[:, cols], preferred_element_type=F32)
            part += jnp.dot(hidden[1], down_b[:, cols], preferred_element_type=F32)
            sums.append(part.reshape(blocks // 2, eight, step))
        both = jnp.stack(paired(*sums), axis=1)
        out_ref[:, :, k * step : (k + 1) * step] = both.reshape(blocks, eight, step).astype(BF16)


def final_body(kept_ref, come_ref, tok_ref, mask_ref, out_ref):
    few, wide = tok_ref.shape
    half = wide // 2
    total = kept_ref[...] + come_ref[...].astype(F32)
    for q in range(2):
        cols = slice(q * half, (q + 1) * half)
        branch = total[q * few : (q + 1) * few]
        kept = mask_ref[:, cols].astype(F32) * branch / KEEP
        out_ref[:, cols] = (tok_ref[:, cols].astype(F32) + kept).astype(BF16)


def cut_body(place_ref, in_hbm, *refs):
    outs, sems = refs[:-1], refs[-1]
    width = outs[0].shape[1]
    pairs = []
    for k, out in enumerate(outs):
        at = lax.rem(place_ref[0] + k, len(outs)) * width
        pairs.append((in_hbm.at[:, pl.ds(pl.multiple_of(at, width), width)], out))
    for copy in brought(pairs, sems):
        copy.wait()


def sum_cut_body(place_ref, *refs, terms):
    total = refs[0][...].astype(F32)
    for ref in refs[1:terms]:
        total = total + ref[...].astype(F32)
    outs, held = refs[terms:-1], refs[-1]
    held[...] = total
    width = outs[0].shape[1]
    for k, out in enumerate(outs):
        at = lax.rem(place_ref[0] + k, len(outs)) * width
        out[...] = held[:, pl.ds(pl.multiple_of(at, width), width)].astype(out.dtype)


def sum_first_body(place_ref, in_ref, kept_ref, sent_ref):
    total = in_ref[0].astype(F32)
    for i in range(1, in_ref.shape[0]):
        total = total + in_ref[i].astype(F32)
    rows = kept_ref.shape[0]
    first = place_ref[0] == 0
    kept_ref[...] = jnp.where(first, total[:rows], total[rows:])
    sent_ref[...] = jnp.where(first, total[rows:], total[:rows]).astype(BF16)


def sum_body(*refs):
    total = refs[0][...].astype(F32)
    for ref in refs[1:-1]:
        total = total + ref[...].astype(F32)
    refs[-1][...] = total


def shape(*dims, dtype=BF16):
    return jax.ShapeDtypeStruct(dims, dtype)


def place(axis):
    return lax.axis_index(axis).astype(jnp.int32).reshape(1)


def passed_on(x, axis, by):
    size = lax.axis_size(axis)
    return lax.ppermute(x, axis, [(i, (i + by) % size) for i in range(size)])


def bucket_over_x(bucket):
    rows, cols = bucket.shape
    nx = lax.axis_size("x")
    cut = call(
        cut_body, (shape(rows, cols // nx),) * nx, place("x"), bucket,
        smem=1, hbm=1, vmem=60, scratch=[pltpu.SemaphoreType.DMA((nx,))],
    )
    return [cut[0]] + [passed_on(cut[k], "x", k) for k in range(1, nx)]


def bucket_cut(terms):
    rows, wide = terms[0].shape
    nh = lax.axis_size("zh")
    return call(
        functools.partial(sum_cut_body, terms=len(terms)),
        (shape(rows, wide // nh),) * nh,
        place("zh"), *terms,
        smem=1, scratch=[pltpu.VMEM((rows, wide), F32)],
    )


def per_device(tokens, norm_gain, gate_weight, up_weight, down_weight, drop_mask, grad_bucket):
    few, wide = tokens.shape
    chips = lax.axis_size(CHIPS)
    units = gate_weight.shape[1]
    blocks = shape(chips, 2 * few, wide // 2)

    gathered = call(
        norm_body, blocks, tokens, norm_gain,
        hbm=2, vmem=60,
        scratch=[
            pltpu.VMEM(tokens.shape, BF16),
            pltpu.VMEM(norm_gain.shape, BF16),
            pltpu.SemaphoreType.DMA((2,)),
        ],
    )
    gathered = lax.all_to_all(gathered, CHIPS, 0, 0, tiled=True)
    bucket = bucket_over_x(grad_bucket[0])
    down_weight, bucket[1] = lax.optimization_barrier((down_weight, bucket[1]))
    weights = []
    for mine in (gate_weight.T, up_weight.T, down_weight):
        weights += [mine, passed_on(mine, "c", 1)]
    cut = bucket_cut(bucket)
    gathered, cut = lax.optimization_barrier((gathered, cut))
    terms = call(
        ffn_body, blocks, gathered, *weights,
        hbm=6,
        scratch=[pltpu.VMEM((units, wide), BF16)] * 6 + [pltpu.SemaphoreType.DMA((6,))],
        vmem=48, flops=12 * chips * few * wide * units, moved=14 * wide * units,
    )
    bucket = [cut[0]] + [passed_on(cut[k], "zh", k) for k in range(1, len(cut))]
    pairs = lax.axis_size(("y", "zb"))
    terms = terms.reshape(pairs, 4 * few, wide // 2)
    terms = lax.all_to_all(terms, ("y", "zb"), 0, 0, tiled=True)
    kept, sent = call(
        sum_first_body,
        (shape(2 * few, wide // 2, dtype=F32), shape(2 * few, wide // 2)),
        place("za"), terms,
        smem=1,
    )
    sent, bucket = lax.optimization_barrier((sent, bucket))
    come = passed_on(sent, "za", 1)
    reduced = call(sum_body, shape(*cut[0].shape, dtype=F32), *bucket)
    mixed = call(final_body, shape(few, wide), kept, come, tokens, drop_mask)
    return (mixed, reduced)


def solution(mesh):
    finer = Mesh(mesh.devices.reshape(4, 3, 8, 2, 2, 2), DP + TENSOR)
    return jax.shard_map(
        per_device,
        mesh=finer,
        in_specs=(
            P(DP + TENSOR, None),
            P(),
            P(None, TENSOR),
            P(None, TENSOR),
            P(TENSOR, None),
            P(DP + TENSOR, None),
            P(DP, TENSOR, None),
        ),
        out_specs=(P(DP + TENSOR, None), P(TENSOR, DP)),
        check_vma=False,
    )
```

```python
import functools

import jax
import jax.numpy as jnp
from jax import lax
from jax.experimental import pallas as pl
from jax.experimental.pallas import tpu as pltpu
from jax.sharding import Mesh
from jax.sharding import PartitionSpec as P

DP = ("x", "zh")
CHIPS = ("y", "zb", "za")
TENSOR = ("y", "za", "zb", "c")
BF16, F32 = jnp.bfloat16, jnp.float32
EPS = 1e-05
KEEP = 0.9


def call(body, outs, *args, smem=0, hbm=0, scratch=(), vmem=16, flops=0, moved=1 << 20):
    whole = pl.BlockSpec(memory_space=pltpu.VMEM)
    specs = [pl.BlockSpec(memory_space=pltpu.SMEM)] * smem
    specs += [whole] * (len(args) - smem - hbm)
    specs += [pl.BlockSpec(memory_space=pltpu.HBM)] * hbm
    return pl.pallas_call(
        body,
        out_shape=outs,
        in_specs=specs,
        out_specs=jax.tree.map(lambda _: whole, outs),
        scratch_shapes=list(scratch),
        compiler_params=pltpu.CompilerParams(vmem_limit_bytes=vmem << 20),
        cost_estimate=pl.CostEstimate(flops=flops, bytes_accessed=moved, transcendentals=0),
    )(*args)


def brought(pairs, sems):
    copies = [pltpu.make_async_copy(a, b, sems.at[i]) for i, (a, b) in enumerate(pairs)]
    for copy in copies:
        copy.start()
    return copies


def norm_body(tok_hbm, gain_hbm, out_ref, tok_ref, gain_ref, sems):
    half = tok_ref.shape[1] // 2
    for copy in brought(((tok_hbm, tok_ref), (gain_hbm, gain_ref)), sems):
        copy.wait()
    inputs = tok_ref[...].astype(F32)
    scale = lax.rsqrt(jnp.mean(inputs * inputs, axis=-1, keepdims=True) + EPS)
    normed = inputs * scale * gain_ref[...].astype(F32)[None, :]
    block = jnp.concatenate([normed[:, :half], normed[:, half:]], axis=0).astype(BF16)
    for i in range(out_ref.shape[0]):
        out_ref[i] = block


def paired(first, second):
    upper = lax.broadcasted_iota(jnp.int32, first.shape, 1) < first.shape[1] // 2
    turn = first.shape[1] // 2
    return (
        jnp.where(upper, first, pltpu.roll(second, turn, 1)),
        jnp.where(upper, pltpu.roll(first, turn, 1), second),
    )


def dot_t(x, w):
    return lax.dot_general(x, w, (((1,), (1,)), ((), ())), preferred_element_type=F32)


def ffn_body(x_ref, *refs):
    sent, out_ref, held, sems = refs[:6], refs[6], refs[7:13], refs[13]
    down_a, down_b = held[4:]
    copies = brought(list(zip(sent, held)), sems)
    blocks, eight, half = x_ref.shape
    rows = blocks * eight // 2
    x = x_ref[...].astype(F32).reshape(blocks // 2, 2, eight, half)
    left, right = (v.reshape(rows, half).astype(BF16) for v in paired(x[:, 0], x[:, 1]))

    def through(at):
        copies[at].wait()
        w_ref = held[at]
        return dot_t(left, w_ref[:, :half]) + dot_t(right, w_ref[:, half:])

    gates = [through(0), through(1)]
    ups = [through(2), through(3)]
    hidden = [(gate / (1.0 + jnp.exp(-gate)) * up).astype(BF16) for gate, up in zip(gates, ups)]
    copies[4].wait()
    copies[5].wait()
    step = min(half, 512)
    for k in range(half // step):
        sums = []
        for cols in (slice(k * step, (k + 1) * step), slice(half + k * step, half + (k + 1) * step)):
            part = jnp.dot(hidden[0], down_a[:, cols], preferred_element_type=F32)
            part += jnp.dot(hidden[1], down_b[:, cols], preferred_element_type=F32)
            sums.append(part.reshape(blocks // 2, eight, step))
        both = jnp.stack(paired(*sums), axis=1)
        out_ref[:, :, k * step : (k + 1) * step] = both.reshape(blocks, eight, step).astype(BF16)


def final_body(kept_ref, come_ref, tok_ref, mask_ref, out_ref):
    few, wide = tok_ref.shape
    half = wide // 2
    total = kept_ref[...] + come_ref[...].astype(F32)
    for q in range(2):
        cols = slice(q * half, (q + 1) * half)
        branch = total[q * few : (q + 1) * few]
        kept = mask_ref[:, cols].astype(F32) * branch / KEEP
        out_ref[:, cols] = (tok_ref[:, cols].astype(F32) + kept).astype(BF16)


def cut_body(place_ref, in_hbm, *refs):
    outs, sems = refs[:-1], refs[-1]
    width = outs[0].shape[1]
    pairs = []
    for k, out in enumerate(outs):
        at = lax.rem(place_ref[0] + k, len(outs)) * width
        pairs.append((in_hbm.at[:, pl.ds(pl.multiple_of(at, width), width)], out))
    for copy in brought(pairs, sems):
        copy.wait()


def sum_cut_body(place_ref, *refs, terms):
    total = refs[0][...].astype(F32)
    for ref in refs[1:terms]:
        total = total + ref[...].astype(F32)
    outs, held = refs[terms:-1], refs[-1]
    held[...] = total
    width = outs[0].shape[1]
    for k, out in enumerate(outs):
        at = lax.rem(place_ref[0] + k, len(outs)) * width
        out[...] = held[:, pl.ds(pl.multiple_of(at, width), width)].astype(out.dtype)


def sum_first_body(place_ref, in_ref, kept_ref, sent_ref):
    total = in_ref[0].astype(F32)
    for i in range(1, in_ref.shape[0]):
        total = total + in_ref[i].astype(F32)
    rows = kept_ref.shape[0]
    first = place_ref[0] == 0
    kept_ref[...] = jnp.where(first, total[:rows], total[rows:])
    sent_ref[...] = jnp.where(first, total[rows:], total[:rows]).astype(BF16)


def sum_body(*refs):
    total = refs[0][...].astype(F32)
    for ref in refs[1:-1]:
        total = total + ref[...].astype(F32)
    refs[-1][...] = total


def shape(*dims, dtype=BF16):
    return jax.ShapeDtypeStruct(dims, dtype)


def place(axis):
    return lax.axis_index(axis).astype(jnp.int32).reshape(1)


def passed_on(x, axis, by):
    size = lax.axis_size(axis)
    return lax.ppermute(x, axis, [(i, (i + by) % size) for i in range(size)])


def bucket_over_x(bucket):
    rows, cols = bucket.shape
    nx = lax.axis_size("x")
    cut = call(
        cut_body, (shape(rows, cols // nx),) * nx, place("x"), bucket,
        smem=1, hbm=1, vmem=60, scratch=[pltpu.SemaphoreType.DMA((nx,))],
    )
    return [cut[0]] + [passed_on(cut[k], "x", k) for k in range(1, nx)]


def bucket_cut(terms):
    rows, wide = terms[0].shape
    nh = lax.axis_size("zh")
    return call(
        functools.partial(sum_cut_body, terms=len(terms)),
        (shape(rows, wide // nh),) * nh,
        place("zh"), *terms,
        smem=1, scratch=[pltpu.VMEM((rows, wide), F32)],
    )


def per_device(tokens, norm_gain, gate_weight, up_weight, down_weight, drop_mask, grad_bucket):
    few, wide = tokens.shape
    chips = lax.axis_size(CHIPS)
    units = gate_weight.shape[1]
    blocks = shape(chips, 2 * few, wide // 2)

    gathered = call(
        norm_body, blocks, tokens, norm_gain,
        hbm=2, vmem=60,
        scratch=[
            pltpu.VMEM(tokens.shape, BF16),
            pltpu.VMEM(norm_gain.shape, BF16),
            pltpu.SemaphoreType.DMA((2,)),
        ],
    )
    gathered = lax.all_to_all(gathered, CHIPS, 0, 0, tiled=True)
    bucket = bucket_over_x(grad_bucket[0])
    down_weight, bucket[1] = lax.optimization_barrier((down_weight, bucket[1]))
    weights = []
    for mine in (gate_weight.T, up_weight.T, down_weight):
        weights += [mine, passed_on(mine, "c", 1)]
    cut = bucket_cut(bucket)
    gathered, cut = lax.optimization_barrier((gathered, cut))
    terms = call(
        ffn_body, blocks, gathered, *weights,
        hbm=6,
        scratch=[pltpu.VMEM((units, wide), BF16)] * 6 + [pltpu.SemaphoreType.DMA((6,))],
        vmem=48, flops=12 * chips * few * wide * units, moved=14 * wide * units,
    )
    bucket = [cut[0]] + [passed_on(cut[k], "zh", k) for k in range(1, len(cut))]
    pairs = lax.axis_size(("y", "zb"))
    terms = terms.reshape(pairs, 4 * few, wide // 2)
    terms = lax.all_to_all(terms, ("y", "zb"), 0, 0, tiled=True)
    kept, sent = call(
        sum_first_body,
        (shape(2 * few, wide // 2, dtype=F32), shape(2 * few, wide // 2)),
        place("za"), terms,
        smem=1,
    )
    sent, bucket[-1] = lax.optimization_barrier((sent, bucket[-1]))
    come = passed_on(sent, "za", 1)
    reduced = call(sum_body, shape(*cut[0].shape, dtype=F32), *bucket)
    mixed = call(final_body, shape(few, wide), kept, come, tokens, drop_mask)
    return (mixed, reduced)


def solution(mesh):
    finer = Mesh(mesh.devices.reshape(4, 3, 8, 2, 2, 2), DP + TENSOR)
    return jax.shard_map(
        per_device,
        mesh=finer,
        in_specs=(
            P(DP + TENSOR, None),
            P(),
            P(None, TENSOR),
            P(None, TENSOR),
            P(TENSOR, None),
            P(DP + TENSOR, None),
            P(DP, TENSOR, None),
        ),
        out_specs=(P(DP + TENSOR, None), P(TENSOR, DP)),
        check_vma=False,
    )
```

```python
import functools

import jax
import jax.numpy as jnp
from jax import lax
from jax.experimental import pallas as pl
from jax.experimental.pallas import tpu as pltpu
from jax.sharding import Mesh
from jax.sharding import PartitionSpec as P

DP = ("x", "zh")
CHIPS = ("y", "zb", "za")
TENSOR = ("y", "za", "zb", "c")
BF16, F32 = jnp.bfloat16, jnp.float32
EPS = 1e-05
KEEP = 0.9


def call(body, outs, *args, smem=0, hbm=0, far_out=False, scratch=(), vmem=16, flops=0, moved=1 << 20):
    whole = pl.BlockSpec(memory_space=pltpu.VMEM)
    specs = [pl.BlockSpec(memory_space=pltpu.SMEM)] * smem
    specs += [whole] * (len(args) - smem - hbm)
    specs += [pl.BlockSpec(memory_space=pltpu.HBM)] * hbm
    return pl.pallas_call(
        body,
        out_shape=outs,
        in_specs=specs,
        out_specs=jax.tree.map(lambda _: pl.BlockSpec(memory_space=pltpu.HBM) if far_out else whole, outs),
        scratch_shapes=list(scratch),
        compiler_params=pltpu.CompilerParams(vmem_limit_bytes=vmem << 20),
        cost_estimate=pl.CostEstimate(flops=flops, bytes_accessed=moved, transcendentals=0),
    )(*args)


def brought(pairs, sems):
    copies = [pltpu.make_async_copy(a, b, sems.at[i]) for i, (a, b) in enumerate(pairs)]
    for copy in copies:
        copy.start()
    return copies


def norm_body(tok_hbm, gain_hbm, out_hbm, tok_ref, gain_ref, block_ref, sems, sent):
    half = tok_ref.shape[1] // 2
    for copy in brought(((tok_hbm, tok_ref), (gain_hbm, gain_ref)), sems):
        copy.wait()
    inputs = tok_ref[...].astype(F32)
    scale = lax.rsqrt(jnp.mean(inputs * inputs, axis=-1, keepdims=True) + EPS)
    normed = inputs * scale * gain_ref[...].astype(F32)[None, :]
    block = jnp.concatenate([normed[:, :half], normed[:, half:]], axis=0).astype(BF16)
    block_ref[...] = block
    pairs = [(block_ref, out_hbm.at[i]) for i in range(out_hbm.shape[0])]
    for copy in brought(pairs, sent):
        copy.wait()


def paired(first, second):
    upper = lax.broadcasted_iota(jnp.int32, first.shape, 1) < first.shape[1] // 2
    turn = first.shape[1] // 2
    return (
        jnp.where(upper, first, pltpu.roll(second, turn, 1)),
        jnp.where(upper, pltpu.roll(first, turn, 1), second),
    )


def dot_t(x, w):
    return lax.dot_general(x, w, (((1,), (1,)), ((), ())), preferred_element_type=F32)


def ffn_body(x_ref, *refs):
    sent, out_ref, held, sems = refs[:6], refs[6], refs[7:13], refs[13]
    down_a, down_b = held[4:]
    copies = brought(list(zip(sent, held)), sems)
    blocks, eight, half = x_ref.shape
    rows = blocks * eight // 2
    x = x_ref[...].astype(F32).reshape(blocks // 2, 2, eight, half)
    left, right = (v.reshape(rows, half).astype(BF16) for v in paired(x[:, 0], x[:, 1]))

    def through(at):
        copies[at].wait()
        w_ref = held[at]
        return dot_t(left, w_ref[:, :half]) + dot_t(right, w_ref[:, half:])

    gates = [through(0), through(1)]
    ups = [through(2), through(3)]
    hidden = [(gate / (1.0 + jnp.exp(-gate)) * up).astype(BF16) for gate, up in zip(gates, ups)]
    copies[4].wait()
    copies[5].wait()
    step = min(half, 512)
    for k in range(half // step):
        sums = []
        for cols in (slice(k * step, (k + 1) * step), slice(half + k * step, half + (k + 1) * step)):
            part = jnp.dot(hidden[0], down_a[:, cols], preferred_element_type=F32)
            part += jnp.dot(hidden[1], down_b[:, cols], preferred_element_type=F32)
            sums.append(part.reshape(blocks // 2, eight, step))
        both = jnp.stack(paired(*sums), axis=1)
        out_ref[:, :, k * step : (k + 1) * step] = both.reshape(blocks, eight, step).astype(BF16)


def final_body(kept_ref, come_ref, tok_ref, mask_ref, out_ref):
    few, wide = tok_ref.shape
    half = wide // 2
    total = kept_ref[...] + come_ref[...].astype(F32)
    for q in range(2):
        cols = slice(q * half, (q + 1) * half)
        branch = total[q * few : (q + 1) * few]
        kept = mask_ref[:, cols].astype(F32) * branch / KEEP
        out_ref[:, cols] = (tok_ref[:, cols].astype(F32) + kept).astype(BF16)


def cut_body(place_ref, in_hbm, *refs):
    outs, sems = refs[:-1], refs[-1]
    width = outs[0].shape[1]
    pairs = []
    for k, out in enumerate(outs):
        at = lax.rem(place_ref[0] + k, len(outs)) * width
        pairs.append((in_hbm.at[:, pl.ds(pl.multiple_of(at, width), width)], out))
    for copy in brought(pairs, sems):
        copy.wait()


def sum_cut_body(place_ref, *refs, terms):
    total = refs[0][...].astype(F32)
    for ref in refs[1:terms]:
        total = total + ref[...].astype(F32)
    outs, held = refs[terms:-1], refs[-1]
    held[...] = total
    width = outs[0].shape[1]
    for k, out in enumerate(outs):
        at = lax.rem(place_ref[0] + k, len(outs)) * width
        out[...] = held[:, pl.ds(pl.multiple_of(at, width), width)].astype(out.dtype)


def sum_first_body(place_ref, in_ref, kept_ref, sent_ref):
    total = in_ref[0].astype(F32)
    for i in range(1, in_ref.shape[0]):
        total = total + in_ref[i].astype(F32)
    rows = kept_ref.shape[0]
    first = place_ref[0] == 0
    kept_ref[...] = jnp.where(first, total[:rows], total[rows:])
    sent_ref[...] = jnp.where(first, total[rows:], total[:rows]).astype(BF16)


def sum_body(*refs):
    total = refs[0][...].astype(F32)
    for ref in refs[1:-1]:
        total = total + ref[...].astype(F32)
    refs[-1][...] = total


def shape(*dims, dtype=BF16):
    return jax.ShapeDtypeStruct(dims, dtype)


def place(axis):
    return lax.axis_index(axis).astype(jnp.int32).reshape(1)


def passed_on(x, axis, by):
    size = lax.axis_size(axis)
    return lax.ppermute(x, axis, [(i, (i + by) % size) for i in range(size)])


def bucket_over_x(bucket):
    rows, cols = bucket.shape
    nx = lax.axis_size("x")
    cut = call(
        cut_body, (shape(rows, cols // nx),) * nx, place("x"), bucket,
        smem=1, hbm=1, vmem=40, scratch=[pltpu.SemaphoreType.DMA((nx,))],
    )
    return [cut[0]] + [passed_on(cut[k], "x", k) for k in range(1, nx)]


def bucket_cut(terms):
    rows, wide = terms[0].shape
    nh = lax.axis_size("zh")
    return call(
        functools.partial(sum_cut_body, terms=len(terms)),
        (shape(rows, wide // nh),) * nh,
        place("zh"), *terms,
        smem=1, scratch=[pltpu.VMEM((rows, wide), F32)],
    )


def per_device(tokens, norm_gain, gate_weight, up_weight, down_weight, drop_mask, grad_bucket):
    few, wide = tokens.shape
    chips = lax.axis_size(CHIPS)
    units = gate_weight.shape[1]
    blocks = shape(chips, 2 * few, wide // 2)

    gathered = call(
        norm_body, blocks, tokens, norm_gain,
        hbm=2, vmem=60, far_out=True,
        scratch=[
            pltpu.VMEM(tokens.shape, BF16),
            pltpu.VMEM(norm_gain.shape, BF16),
            pltpu.VMEM((2 * few, wide // 2), BF16),
            pltpu.SemaphoreType.DMA((2,)),
            pltpu.SemaphoreType.DMA((chips,)),
        ],
    )
    gathered = lax.all_to_all(gathered, CHIPS, 0, 0, tiled=True)
    bucket = bucket_over_x(grad_bucket[0])
    down_weight, bucket[1] = lax.optimization_barrier((down_weight, bucket[1]))
    weights = []
    for mine in (gate_weight.T, up_weight.T, down_weight):
        weights += [mine, passed_on(mine, "c", 1)]
    cut = bucket_cut(bucket)
    gathered, cut = lax.optimization_barrier((gathered, cut))
    terms = call(
        ffn_body, blocks, gathered, *weights,
        hbm=6,
        scratch=[pltpu.VMEM((units, wide), BF16)] * 6 + [pltpu.SemaphoreType.DMA((6,))],
        vmem=48, flops=12 * chips * few * wide * units, moved=14 * wide * units,
    )
    bucket = [cut[0]] + [passed_on(cut[k], "zh", k) for k in range(1, len(cut))]
    pairs = lax.axis_size(("y", "zb"))
    terms = terms.reshape(pairs, 4 * few, wide // 2)
    terms = lax.all_to_all(terms, ("y", "zb"), 0, 0, tiled=True)
    kept, sent = call(
        sum_first_body,
        (shape(2 * few, wide // 2, dtype=F32), shape(2 * few, wide // 2)),
        place("za"), terms,
        smem=1,
    )
    sent, bucket[-1] = lax.optimization_barrier((sent, bucket[-1]))
    come = passed_on(sent, "za", 1)
    reduced = call(sum_body, shape(*cut[0].shape, dtype=F32), *bucket)
    mixed = call(final_body, shape(few, wide), kept, come, tokens, drop_mask)
    return (mixed, reduced)


def solution(mesh):
    finer = Mesh(mesh.devices.reshape(4, 3, 8, 2, 2, 2), DP + TENSOR)
    return jax.shard_map(
        per_device,
        mesh=finer,
        in_specs=(
            P(DP + TENSOR, None),
            P(),
            P(None, TENSOR),
            P(None, TENSOR),
            P(TENSOR, None),
            P(DP + TENSOR, None),
            P(DP, TENSOR, None),
        ),
        out_specs=(P(DP + TENSOR, None), P(TENSOR, DP)),
        check_vma=False,
    )
```
